32 devices in a mesh: scen: 4 (over z), net: 8 (over y, x, core).
Axes of the slice: x: 2, y: 2, z: 4, core: 2. Of those that a mesh axis runs over, the one named last changes fastest.
Arguments:
- coupling: bfloat16 [768, 64, 320], P('net'), may hold values from -0.3125 to 0.3125
- tie_blocks: bfloat16 [1024, 64, 128], P('net'), may hold values from -0.5 to 0.5
- w_pattern: int32 [768, 4], P('net'), may hold values from 0 to 127
- link_pattern: int32 [768], P('net'), may hold values from 0 to 127
- left_bounds: int32 [1024], P('net'), may hold values from 0 to 127
- right_bounds: int32 [1024], P('net'), may hold values from 0 to 127
- block_counts: int32 [8], P('net'), may hold values from 48 to 96, as said below
- commit_cost: float32 [1024, 64], P('net'), may hold values from -3 to 3
- dispatch_cost: float32 [1024, 64], P('net'), may hold values from -6 to 6
- demand: float32 [768, 64], P('net'), may hold values from -6 to 6
- wind_error: bfloat16 [768, 64, 512], P('net', None, 'scen'), may hold values from -3 to 3
- commit_start: float32 [1024, 64], P('net'), may hold values from 0 to 1
- dispatch_start: float32 [1024, 64, 512], P('net', None, 'scen'), may hold values from 0 to 2
- dual_start: float32 [768, 64, 512], P('net', None, 'scen'), may hold values from -8 to 8
- tie_start: float32 [1024, 64, 512], P('net', None, 'scen'), may hold values from -6 to 6
Outputs:
- commit_out: float32 [1024, 64], P('net')
- dispatch_out: float32 [1024, 64, 512], P('net', None, 'scen')
- dual_out: float32 [768, 64, 512], P('net', None, 'scen')
- tie_out: float32 [1024, 64, 512], P('net', None, 'scen')
The draws below stay inside these ranges and needn't reach their ends.
Inputs may be any that keep to these rules, and one draw needn't show every extreme that they name: `block_counts`: some partition has all 96 row blocks active.
All inputs are finite; a program needn't handle non-finite values.
Results may differ from the reference program's by a relative error of at most 0.0035.
Values may be sent and summed in bfloat16 or wider, within the bound.
A program may use at most 192 MiB of HBM per device.

```python
import jax
import jax.numpy as jnp
from jax import lax

BLK = 64
KW = 4
ITERS = 2
YB = 128
RB = 96
XB = 128
BB = 128
PARTS_SIZE = 8
SCEN = 512
NYB = 1024
NRB = 768
NXB = 1024
NBB = 1024


def draw_block_counts(key, part):
    key_a, key_b = jax.random.split(jax.random.fold_in(key, 11))
    drawn = jax.random.randint(key_a, (PARTS_SIZE,), RB // 2, RB + 1)
    fullest = jax.random.randint(key_b, (), 0, PARTS_SIZE)
    return jnp.where(jnp.arange(PARTS_SIZE) == fullest, RB, drawn).astype(jnp.int32)


def draw_dual_start(key, part):
    key_a, key_b = jax.random.split(jax.random.fold_in(key, 23), 2)
    common = jax.random.normal(key_a, (NRB, BLK, 1), jnp.float32)
    values = common + 0.5 * jax.random.normal(key_b, (NRB, BLK, SCEN), jnp.float32)
    return jnp.clip(values, -8.0, 8.0)


def place_ends(array, rng, least, top_value):
    longest = array.shape.index(max(array.shape))
    spots = []
    for shift in (0, 1):
        where = [jax.random.randint(jax.random.fold_in(rng, axis), (), 0, length) for axis, length in enumerate(array.shape)]
        where[longest] = (where[longest] + shift) % array.shape[longest]
        spots.append(tuple(where))
    return array.at[spots[0]].set(least).at[spots[1]].set(top_value)


def steps_of(stream_key, dims, cuts, least, high):
    factor_of, own = 1.0, jax.random.fold_in(stream_key, 6)
    for position, shards_of in cuts:
        draws = jnp.exp(jax.random.uniform(jax.random.fold_in(own, position), (shards_of,), jnp.float32, least / len(cuts), high / len(cuts)))
        factor_of = factor_of * jnp.repeat(draws, dims[position] // shards_of).reshape([-1 if axis == position else 1 for axis in range(len(dims))])
    return factor_of


def normal_values(stream_key, dims, scale, most, shards=(), kind=jnp.bfloat16):
    values = scale * jax.random.normal(stream_key, dims, jnp.float32)
    if shards:
        values = values * steps_of(stream_key, dims, shards, -0.22, 0.18)
    return jnp.clip(values, -most, most).astype(kind)


def setup_inputs(seed: int = 0) -> dict:
    splits = jax.random.split(jax.random.key(seed), 16)
    return {
        "coupling": normal_values(splits[0], (NRB, BLK, (KW + 1) * BLK), ((KW + 1) * BLK) ** -0.5, 0.3125, ((0, 8),)),
        "tie_blocks": normal_values(splits[1], (NBB, BLK, 2 * BLK), (2 * BLK) ** -0.5, 0.5, ((0, 8),)),
        "w_pattern": place_ends(jax.random.randint(splits[2], (NRB, KW), 0, YB), jax.random.fold_in(splits[2], 1), 0, YB - 1).astype(jnp.int32),
        "link_pattern": place_ends(jax.random.randint(splits[3], (NRB,), 0, XB), jax.random.fold_in(splits[3], 1), 0, XB - 1).astype(jnp.int32),
        "left_bounds": place_ends(jax.random.randint(splits[4], (NBB,), 0, YB), jax.random.fold_in(splits[4], 1), 0, YB - 1).astype(jnp.int32),
        "right_bounds": place_ends(jax.random.randint(splits[5], (NBB,), 0, YB), jax.random.fold_in(splits[5], 1), 0, YB - 1).astype(jnp.int32),
        "block_counts": draw_block_counts(jax.random.fold_in(splits[15], 71), 0),
        "commit_cost": normal_values(splits[7], (NXB, BLK), 0.5, 3.0, ((0, 8),), jnp.float32),
        "dispatch_cost": normal_values(splits[8], (NYB, BLK), 1.0, 6.0, ((0, 8),), jnp.float32),
        "demand": normal_values(splits[9], (NRB, BLK), 1.0, 6.0, ((0, 8),), jnp.float32),
        "wind_error": normal_values(splits[10], (NRB, BLK, SCEN), 0.5, 3.0, ((0, 8), (2, 4))),
        "commit_start": jnp.clip(1.0 * jax.random.uniform(splits[11], (NXB, BLK), jnp.float32) ** steps_of(splits[11], (NXB, BLK), ((0, 8),), -0.2, 0.2), 0.0, 1.0),
        "dispatch_start": jnp.clip(2.0 * jax.random.uniform(splits[12], (NYB, BLK, SCEN), jnp.float32) ** steps_of(splits[12], (NYB, BLK, SCEN), ((0, 8), (2, 4)), -0.2, 0.2), 0.0, 2.0),
        "dual_start": draw_dual_start(jax.random.fold_in(splits[15], 71), 0),
        "tie_start": normal_values(splits[14], (NBB, BLK, SCEN), 1.0, 6.0, ((0, 8), (2, 4)), jnp.float32),
    }


def forward_blocks(block_mats, stacked):
    block_count = block_mats.shape[0]
    joined = stacked.astype(jnp.float32).reshape(block_count, -1, stacked.shape[-1])
    return jnp.einsum('roj,rjs->ros', block_mats.astype(jnp.float32), joined)


def backward_blocks(block_mats, dual_rows, width):
    block_count = block_mats.shape[0]
    result = jnp.einsum('roj,ros->rjs', block_mats.astype(jnp.float32), dual_rows.astype(jnp.float32))
    return result.reshape(block_count, width, BLK, -1)


def reference(coupling, tie_blocks, w_pattern, link_pattern, left_bounds, right_bounds, block_counts, commit_cost, dispatch_cost, demand, wind_error, commit_start, dispatch_start, dual_start, tie_start):
    part_count = PARTS_SIZE
    active = (jnp.arange(RB)[None, :] < block_counts[:, None]).astype(jnp.float32).reshape(NRB, 1, 1)
    live_tie = jnp.repeat((jnp.arange(part_count) < part_count - 1).astype(jnp.float32), BB)[:, None, None]
    weight_parts = coupling.reshape(part_count, RB, BLK, (KW + 1) * BLK)
    pattern_parts = w_pattern.reshape(part_count, RB, KW)
    link_parts = link_pattern.reshape(part_count, RB)
    tie_parts = tie_blocks.reshape(part_count, BB, BLK, 2 * BLK)
    left_parts = left_bounds.reshape(part_count, BB)
    right_parts = right_bounds.reshape(part_count, BB)
    cost_col = dispatch_cost[:, :, None]
    target = demand[:, :, None] + wind_error.astype(jnp.float32)
    first_now = commit_start
    second_now = dispatch_start
    dual_now = dual_start * active
    tie_now = tie_start * live_tie
    for iteration in range(ITERS):
        dual_half = dual_now.astype(jnp.bfloat16).reshape(part_count, RB, BLK, -1)
        tie_half = tie_now.astype(jnp.bfloat16).reshape(part_count, BB, BLK, -1)

        def backward_part(inputs):
            weight_p, pattern_p, link_p, dual_p = inputs
            block_terms = backward_blocks(weight_p, dual_p, KW + 1)
            grad_second = jax.ops.segment_sum(block_terms[:, :KW].reshape(RB * KW, BLK, -1), pattern_p.reshape(-1), num_segments=YB)
            link_terms = jnp.sum(block_terms[:, KW], axis=2) / SCEN
            grad_first = jax.ops.segment_sum(link_terms, link_p, num_segments=XB)
            return grad_second, grad_first

        grad_second, grad_first = lax.map(backward_part, (weight_parts, pattern_parts, link_parts, dual_half))
        tie_terms = jax.vmap(lambda mats_p, duals_p: backward_blocks(mats_p, duals_p, 2))(tie_parts, tie_half)
        own_terms = tie_terms[:, :, 0]
        left_terms = tie_terms[:, :, 1]
        left_terms = jnp.concatenate([jnp.zeros_like(left_terms[:1]), left_terms[:-1]], axis=0)
        add_own = jax.vmap(lambda vals, idx: jax.ops.segment_sum(vals, idx, num_segments=YB))(own_terms, right_parts)
        add_left = jax.vmap(lambda vals, idx: jax.ops.segment_sum(vals, idx, num_segments=YB))(left_terms, left_parts)
        grad_second = (grad_second + add_own + add_left).reshape(NYB, BLK, -1)
        grad_first = grad_first.reshape(NXB, BLK)
        first_next = jnp.clip(first_now - 1.0 * (commit_cost - grad_first), 0.0, 1.0)
        second_next = jnp.maximum(second_now - 0.4 * (cost_col - grad_second), 0.0)
        first_bar = (2.0 * first_next - first_now).astype(jnp.bfloat16).reshape(part_count, XB, BLK)
        second_bar = (2.0 * second_next - second_now).astype(jnp.bfloat16).reshape(part_count, YB, BLK, -1)

        def forward_part(inputs):
            weight_p, pattern_p, link_p, second_p, first_p = inputs
            gathered = second_p[pattern_p]
            linked = jnp.broadcast_to(first_p[link_p][:, None, :, None], (RB, 1, BLK, gathered.shape[3]))
            return forward_blocks(weight_p, jnp.concatenate([gathered, linked], axis=1))

        coupled = lax.map(forward_part, (weight_parts, pattern_parts, link_parts, second_bar, first_bar)).reshape(NRB, BLK, -1)
        own_rows = jax.vmap(lambda vals, idx: vals[idx])(second_bar, right_parts)
        next_rows = jax.vmap(lambda vals, idx: vals[idx])(second_bar, left_parts)
        next_rows = jnp.concatenate([next_rows[1:], jnp.zeros_like(next_rows[:1])], axis=0)
        tie_inputs = jnp.stack([own_rows, next_rows], axis=2)
        tie_rows = jax.vmap(forward_blocks)(tie_parts, tie_inputs).reshape(NBB, BLK, -1)
        dual_now = (dual_now + 0.4 * (target - coupled)) * active
        tie_now = (tie_now - 0.4 * tie_rows) * live_tie
        first_now = first_next
        second_now = second_next
    return first_now, second_now, dual_now, tie_now
```

```python
import jax
import jax.numpy as jnp
from jax import lax
from jax.experimental import pallas as pl
from jax.experimental.pallas import tpu as pltpu
from jax.sharding import PartitionSpec as P

BLK = 64
KW = 4
ITERS = 2
UNROLL = 4

primal_step = 0.4
first_step = 1.0
dual_step = 0.4

VMEM = pl.BlockSpec(memory_space=pltpu.VMEM)
SMEM = pl.BlockSpec(memory_space=pltpu.SMEM)
F32 = jnp.float32
BF16 = jnp.bfloat16


def from_behind(value, axis, by):
    devices = lax.axis_size(axis)
    pairs = [(i, i + by) for i in range(devices) if 0 <= i + by < devices]
    return lax.ppermute(value, axis, pairs)


def local_call(kernel, out_shape, in_specs, flops, moved):
    return pl.pallas_call(
        kernel,
        out_shape=out_shape,
        in_specs=in_specs,
        out_specs=jax.tree.map(lambda _: VMEM, out_shape),
        compiler_params=pltpu.CompilerParams(vmem_limit_bytes=48 * 2**20),
        cost_estimate=pl.CostEstimate(flops=flops, bytes_accessed=moved, transcendentals=0),
    )


def rows_loop(count, step):
    def chunk(c, carry):
        step([c * UNROLL + u for u in range(UNROLL)])
        return carry

    lax.fori_loop(0, count // UNROLL, chunk, 0)


def transposed_dot(a, b):
    return lax.dot_general(a, b, (((0,), (0,)), ((), ())), preferred_element_type=F32)


def left_terms_kernel(live, tie, mu, terms):
    def step(rows):
        for j in rows:
            half = (mu[j] * live[0]).astype(BF16)
            terms[j] = transposed_dot(tie[j], half)[BLK:].astype(BF16)

    rows_loop(tie.shape[0], step)


def gradient_kernel(live, count, pattern, link, right, coupling, tie, lam, mu, grad, grad_first):
    grad[...] = jnp.zeros_like(grad)
    grad_first[...] = jnp.zeros_like(grad_first)
    ones = jnp.ones((8, lam.shape[2]), BF16)

    def tie_step(rows):
        parts = [transposed_dot(tie[j], (mu[j] * live[0]).astype(BF16))[:BLK] for j in rows]
        for j, part in zip(rows, parts):
            grad[right[j]] += part

    rows_loop(tie.shape[0], tie_step)

    def row_step(rows):
        halves = [jnp.where(r < count[0], lam[r], 0.0).astype(BF16) for r in rows]
        parts = [transposed_dot(coupling[r, :, : KW * BLK], h) for r, h in zip(rows, halves)]
        firsts = []
        for r, h in zip(rows, halves):
            total = lax.dot_general(ones, h, (((1,), (1,)), ((), ())), preferred_element_type=F32)
            firsts.append(
                lax.dot_general(
                    total,
                    coupling[r, :, KW * BLK :].astype(F32),
                    (((1,), (0,)), ((), ())),
                    precision=lax.Precision.HIGHEST,
                    preferred_element_type=F32,
                )
            )
        for r, part, first in zip(rows, parts, firsts):
            for k in range(KW):
                grad[pattern[r * KW + k]] += part[k * BLK : (k + 1) * BLK]
            grad_first[pl.ds(link[r], 1), :] += first[:1]

    rows_loop(coupling.shape[0], row_step)


def primal_kernel(left, received, grad, cost, second, next_left, second_next, second_bar, sent, total):
    total[...] = grad[...]

    def add_step(rows):
        for j in rows:
            total[left[j]] += received[j].astype(F32)

    rows_loop(received.shape[0], add_step)

    def move_step(rows):
        for b in rows:
            now = second[b]
            new = jnp.maximum(now - primal_step * (cost[b] - total[b]), 0.0)
            second_next[b] = new
            second_bar[b] = (2.0 * new - now).astype(BF16)

    rows_loop(second.shape[0], move_step)

    def gather_step(rows):
        for j in rows:
            sent[j] = second_bar[left[j]]

    rows_loop(received.shape[0], gather_step)


def dual_kernel(live, count, pattern, link, right, coupling, tie, bar, first, target, lam, mu, lam_next, mu_part):
    def row_step(rows):
        for r in rows:
            gathered = [bar[pattern[r * KW + k]] for k in range(KW)] + [first[link[r]]]
            coupled = jnp.dot(coupling[r], jnp.concatenate(gathered, axis=0), preferred_element_type=F32)
            new = lam[r] + dual_step * (target[r] - coupled)
            lam_next[r] = jnp.where(r < count[0], new, 0.0)

    rows_loop(coupling.shape[0], row_step)

    def tie_step(rows):
        for j in rows:
            own = jnp.dot(tie[j, :, :BLK], bar[right[j]], preferred_element_type=F32)
            mu_part[j] = mu[j] * live[0] - dual_step * own

    rows_loop(tie.shape[0], tie_step)


def tie_kernel(live, tie, mu_part, arrived, mu_next, *terms):
    def step(rows):
        for j in rows:
            block = tie[j]
            new = (
                mu_part[j]
                - dual_step * jnp.dot(block[:, BLK:], arrived[j], preferred_element_type=F32)
            ) * live[0]
            mu_next[j] = new
            if terms:
                terms[0][j] = transposed_dot(block, new.astype(BF16))[BLK:].astype(BF16)

    rows_loop(tie.shape[0], step)


def primal_call(left, received, grad, cost, second):
    shape = second.shape

    def kernel(left, received, grad, cost, second, second_next, second_bar, sent, total):
        primal_kernel(left, received, grad, cost, second, None, second_next, second_bar, sent, total)

    return pl.pallas_call(
        kernel,
        out_shape=(
            jax.ShapeDtypeStruct(shape, F32),
            jax.ShapeDtypeStruct(shape, BF16),
            jax.ShapeDtypeStruct(received.shape, BF16),
        ),
        in_specs=[SMEM] + [VMEM] * 4,
        out_specs=(VMEM,) * 3,
        scratch_shapes=[pltpu.VMEM(shape, F32)],
        compiler_params=pltpu.CompilerParams(vmem_limit_bytes=48 * 2**20),
        cost_estimate=pl.CostEstimate(flops=10**7, bytes_accessed=25 * 10**6, transcendentals=0),
    )(left, received, grad, cost, second)


def body(
    coupling,
    tie_blocks,
    w_pattern,
    link_pattern,
    left_bounds,
    right_bounds,
    block_counts,
    commit_cost,
    dispatch_cost,
    demand,
    wind_error,
    commit_start,
    dispatch_start,
    dual_start,
    tie_start,
):
    scen_dev = dispatch_start.shape[2]
    scen_total = scen_dev * lax.axis_size("scen")
    second_shape = dispatch_start.shape
    tie_shape = tie_start.shape
    live = (lax.axis_index("net") < lax.axis_size("net") - 1).astype(F32).reshape(1)
    pattern = w_pattern.reshape(-1)
    cost = jnp.broadcast_to(dispatch_cost[:, :, None], second_shape)
    target = demand[:, :, None] + wind_error.astype(F32)
    first_now = commit_start
    second_now = dispatch_start
    dual_now = dual_start
    tie_now = tie_start
    terms = local_call(
        left_terms_kernel, jax.ShapeDtypeStruct(tie_shape, BF16), [SMEM, VMEM, VMEM], 3 * 10**8, 10**7
    )(live, tie_blocks, tie_start)
    for iteration in range(ITERS):
        received = from_behind(terms, "net", 1)
        grad, grad_part = local_call(
            gradient_kernel,
            (jax.ShapeDtypeStruct(second_shape, F32), jax.ShapeDtypeStruct(first_now.shape, F32)),
            [SMEM] * 5 + [VMEM] * 4,
            8 * 10**8,
            18 * 10**6,
        )(live, block_counts, pattern, link_pattern, right_bounds, coupling, tie_blocks, dual_now, tie_now)
        grad_first = lax.psum((grad_part / scen_total).astype(BF16), "scen").astype(F32)
        first_next = jnp.clip(first_now - first_step * (commit_cost - grad_first), 0.0, 1.0)
        first_bar = (2.0 * first_next - first_now).astype(BF16)
        first_wide = jnp.broadcast_to(first_bar[:, :, None], first_bar.shape + (scen_dev,))
        second_next, second_bar, sent = primal_call(left_bounds, received, grad, cost, second_now)
        arrived = from_behind(sent, "net", -1)
        dual_now, tie_part = local_call(
            dual_kernel,
            (jax.ShapeDtypeStruct(dual_start.shape, F32), jax.ShapeDtypeStruct(tie_shape, F32)),
            [SMEM] * 5 + [VMEM] * 7,
            8 * 10**8,
            30 * 10**6,
        )(
            live, block_counts, pattern, link_pattern, right_bounds,
            coupling, tie_blocks, second_bar, first_wide, target, dual_now, tie_now,
        )
        more = iteration < ITERS - 1
        outs = (jax.ShapeDtypeStruct(tie_shape, F32),)
        if more:
            outs += (jax.ShapeDtypeStruct(tie_shape, BF16),)
        got = local_call(tie_kernel, outs, [SMEM] + [VMEM] * 3, 4 * 10**8, 15 * 10**6)(
            live, tie_blocks, tie_part, arrived
        )
        tie_now = got[0]
        if more:
            terms = got[1]
        first_now = first_next
        second_now = second_next
    return (first_now, second_now, dual_now, tie_now)


def solution(mesh):
    return jax.shard_map(
        body,
        mesh=mesh,
        in_specs=(
            P("net", None, None),
            P("net", None, None),
            P("net", None),
            P("net"),
            P("net"),
            P("net"),
            P("net"),
            P("net", None),
            P("net", None),
            P("net", None),
            P("net", None, "scen"),
            P("net", None),
            P("net", None, "scen"),
            P("net", None, "scen"),
            P("net", None, "scen"),
        ),
        out_specs=(
            P("net", None),
            P("net", None, "scen"),
            P("net", None, "scen"),
            P("net", None, "scen"),
        ),
        check_vma=False,
    )
```

```python
import jax
import jax.numpy as jnp
from jax import lax
from jax.experimental import pallas as pl
from jax.experimental.pallas import tpu as pltpu
from jax.sharding import PartitionSpec as P

BLK = 64
KW = 4
ITERS = 2
UNROLL = 4
STEPS = 8

primal_step = 0.4
first_step = 1.0
dual_step = 0.4

VMEM = pl.BlockSpec(memory_space=pltpu.VMEM)
SMEM = pl.BlockSpec(memory_space=pltpu.SMEM)
F32 = jnp.float32
BF16 = jnp.bfloat16


def from_behind(value, axis, by):
    devices = lax.axis_size(axis)
    pairs = [(i, i + by) for i in range(devices) if 0 <= i + by < devices]
    return lax.ppermute(value, axis, pairs)


def sum_over_scen(value):
    devices = lax.axis_size("scen")
    total = value.astype(F32)
    for by in range(1, devices):
        pairs = [(i, (i + by) % devices) for i in range(devices)]
        total = total + lax.ppermute(value, "scen", pairs).astype(F32)
    return total


def per_step(shape):
    return pl.BlockSpec((shape[0] // STEPS,) + shape[1:], lambda i: (i, 0, 0))


def resident(shape):
    return pl.BlockSpec(shape, lambda i: (0, 0, 0))


def stepped_call(kernel, out_shape, in_specs, out_specs, flops, moved):
    return pl.pallas_call(
        kernel,
        grid=(STEPS,),
        out_shape=out_shape,
        in_specs=in_specs,
        out_specs=out_specs,
        compiler_params=pltpu.CompilerParams(vmem_limit_bytes=48 * 2**20),
        cost_estimate=pl.CostEstimate(flops=flops, bytes_accessed=moved, transcendentals=0),
    )


def rows_loop(count, step, unroll=UNROLL):
    def chunk(c, carry):
        step([c * unroll + u for u in range(unroll)])
        return carry

    lax.fori_loop(0, count // unroll, chunk, 0)


def transposed_dot(a, b):
    return lax.dot_general(a, b, (((0,), (0,)), ((), ())), preferred_element_type=F32)


def zero_first(*refs):
    @pl.when(pl.program_id(0) == 0)
    def _():
        for ref in refs:
            ref[...] = jnp.zeros_like(ref)


def start_terms_kernel(live, right, tie, mu, terms, own):
    base = pl.program_id(0) * tie.shape[0]
    zero_first(own)

    def step(rows):
        parts = [transposed_dot(tie[j], (mu[j] * live[0]).astype(BF16)) for j in rows]
        for j, part in zip(rows, parts):
            terms[j] = part[BLK:].astype(BF16)
            own[right[base + j]] += part[:BLK]

    rows_loop(tie.shape[0], step)


def recourse_kernel(count, pattern, link, coupling, lam, grad, grad_first):
    base = pl.program_id(0) * coupling.shape[0]
    zero_first(grad, grad_first)

    def step(rows):
        halves = [jnp.where(base + r < count[0], lam[r], 0.0).astype(BF16) for r in rows]
        parts = [transposed_dot(coupling[r], h) for r, h in zip(rows, halves)]
        for r, part in zip(rows, parts):
            for k in range(KW):
                grad[pattern[(base + r) * KW + k]] += part[k * BLK : (k + 1) * BLK]
            grad_first[link[base + r]] += part[KW * BLK :]

    rows_loop(coupling.shape[0], step)


def primal_kernel(left, received, grad, own, cost, second, second_next, second_bar, sent, total):
    total[...] = grad[...] + own[...]

    def add_step(rows):
        for j in rows:
            total[left[j]] += received[j].astype(F32)

    rows_loop(received.shape[0], add_step)

    def move_step(rows):
        news = []
        for b in rows:
            now = second[b]
            new = jnp.maximum(now - primal_step * (cost[b] - total[b]), 0.0)
            news.append((new, (2.0 * new - now).astype(BF16)))
        for b, (new, bar) in zip(rows, news):
            second_next[b] = new
            second_bar[b] = bar

    rows_loop(second.shape[0], move_step)

    def gather_step(rows):
        picked = [second_bar[left[j]] for j in rows]
        for j, block in zip(rows, picked):
            sent[j] = block

    rows_loop(received.shape[0], gather_step, 8)


def dual_kernel(count, pattern, link, coupling, bar, first, target, lam, lam_next):
    base = pl.program_id(0) * coupling.shape[0]

    def step(rows):
        news = []
        for r in rows:
            at = base + r
            gathered = [bar[pattern[at * KW + k]] for k in range(KW)] + [first[link[at]]]
            coupled = jnp.dot(coupling[r], jnp.concatenate(gathered, axis=0), preferred_element_type=F32)
            new = lam[r] + dual_step * (target[r] - coupled)
            news.append(jnp.where(at < count[0], new, 0.0))
        for r, new in zip(rows, news):
            lam_next[r] = new

    rows_loop(coupling.shape[0], step)


def tie_kernel(live, right, tie, bar, arrived, mu, mu_next, *more):
    base = pl.program_id(0) * tie.shape[0]
    if more:
        zero_first(more[1])

    def step(rows):
        news = []
        for j in rows:
            stacked = jnp.concatenate([bar[right[base + j]], arrived[j]], axis=0)
            product = jnp.dot(tie[j], stacked, preferred_element_type=F32)
            news.append((mu[j] - dual_step * product) * live[0])
        parts = [transposed_dot(tie[j], new.astype(BF16)) for j, new in zip(rows, news)] if more else []
        for j, new in zip(rows, news):
            mu_next[j] = new
        for j, part in zip(rows, parts):
            more[0][j] = part[BLK:].astype(BF16)
            more[1][right[base + j]] += part[:BLK]

    rows_loop(tie.shape[0], step)


def primal_call(left, received, grad, own, cost, second):
    shape = second.shape
    return pl.pallas_call(
        primal_kernel,
        out_shape=(
            jax.ShapeDtypeStruct(shape, F32),
            jax.ShapeDtypeStruct(shape, BF16),
            jax.ShapeDtypeStruct(received.shape, BF16),
        ),
        in_specs=[SMEM] + [VMEM] * 5,
        out_specs=(VMEM,) * 3,
        scratch_shapes=[pltpu.VMEM(shape, F32)],
        compiler_params=pltpu.CompilerParams(vmem_limit_bytes=48 * 2**20),
        cost_estimate=pl.CostEstimate(flops=10**7, bytes_accessed=25 * 10**6, transcendentals=0),
    )(left, received, grad, own, cost, second)


def body(
    coupling,
    tie_blocks,
    w_pattern,
    link_pattern,
    left_bounds,
    right_bounds,
    block_counts,
    commit_cost,
    dispatch_cost,
    demand,
    wind_error,
    commit_start,
    dispatch_start,
    dual_start,
    tie_start,
):
    scen_dev = dispatch_start.shape[2]
    scen_total = scen_dev * lax.axis_size("scen")
    second_shape = dispatch_start.shape
    tie_shape = tie_start.shape
    wide_shape = commit_start.shape + (scen_dev,)
    live = (lax.axis_index("net") < lax.axis_size("net") - 1).astype(F32).reshape(1)
    pattern = w_pattern.reshape(-1)
    cost = jnp.broadcast_to(dispatch_cost[:, :, None], second_shape)
    target = demand[:, :, None] + wind_error.astype(F32)
    first_now = commit_start
    second_now = dispatch_start
    dual_now = dual_start
    tie_now = tie_start
    second_f32 = jax.ShapeDtypeStruct(second_shape, F32)
    tie_f32 = jax.ShapeDtypeStruct(tie_shape, F32)
    tie_bf16 = jax.ShapeDtypeStruct(tie_shape, BF16)
    dual_f32 = jax.ShapeDtypeStruct(dual_start.shape, F32)
    ties, rows = per_step(tie_shape), per_step(dual_start.shape)
    tie_mats, row_mats = per_step(tie_blocks.shape), per_step(coupling.shape)
    seconds, wides = resident(second_shape), resident(wide_shape)
    terms, own = stepped_call(
        start_terms_kernel,
        (tie_bf16, second_f32),
        [SMEM, SMEM, tie_mats, ties],
        (ties, seconds),
        3 * 10**8,
        13 * 10**6,
    )(live, right_bounds, tie_blocks, tie_start)
    for iteration in range(ITERS):
        received = from_behind(terms, "net", 1)
        grad, grad_wide = stepped_call(
            recourse_kernel,
            (second_f32, jax.ShapeDtypeStruct(wide_shape, F32)),
            [SMEM] * 3 + [row_mats, rows],
            (seconds, wides),
            5 * 10**8,
            16 * 10**6,
        )(block_counts, pattern, link_pattern, coupling, dual_now)
        grad_first = sum_over_scen((jnp.sum(grad_wide, axis=2) / scen_total).astype(BF16))
        second_next, second_bar, sent = primal_call(left_bounds, received, grad, own, cost, second_now)
        sent, grad_first = lax.optimization_barrier((sent, grad_first))
        arrived = from_behind(sent, "net", -1)
        first_next = jnp.clip(first_now - first_step * (commit_cost - grad_first), 0.0, 1.0)
        first_bar = (2.0 * first_next - first_now).astype(BF16)
        first_wide = jnp.broadcast_to(first_bar[:, :, None], wide_shape)
        dual_now = stepped_call(
            dual_kernel,
            dual_f32,
            [SMEM] * 3 + [row_mats, seconds, wides, rows, rows],
            rows,
            5 * 10**8,
            18 * 10**6,
        )(block_counts, pattern, link_pattern, coupling, second_bar, first_wide, target, dual_now)
        arrived, dual_now = lax.optimization_barrier((arrived, dual_now))
        more = iteration < ITERS - 1
        got = stepped_call(
            tie_kernel,
            (tie_f32, tie_bf16, second_f32) if more else (tie_f32,),
            [SMEM, SMEM, tie_mats, seconds, ties, ties],
            (ties, ties, seconds) if more else (ties,),
            6 * 10**8,
            18 * 10**6,
        )(live, right_bounds, tie_blocks, second_bar, arrived, tie_now)
        tie_now = got[0]
        if more:
            terms, own = got[1:]
        first_now = first_next
        second_now = second_next
    return (first_now, second_now, dual_now, tie_now)


def solution(mesh):
    return jax.shard_map(
        body,
        mesh=mesh,
        in_specs=(
            P("net", None, None),
            P("net", None, None),
            P("net", None),
            P("net"),
            P("net"),
            P("net"),
            P("net"),
            P("net", None),
            P("net", None),
            P("net", None),
            P("net", None, "scen"),
            P("net", None),
            P("net", None, "scen"),
            P("net", None, "scen"),
            P("net", None, "scen"),
        ),
        out_specs=(
            P("net", None),
            P("net", None, "scen"),
            P("net", None, "scen"),
            P("net", None, "scen"),
        ),
        check_vma=False,
    )
```

```python
import jax
import jax.numpy as jnp
from jax import lax
from jax.experimental import pallas as pl
from jax.experimental.pallas import tpu as pltpu
from jax.sharding import PartitionSpec as P

BLK = 64
KW = 4
ITERS = 2
UNROLL = 32
STEPS = 4

primal_step = 0.4
first_step = 1.0
dual_step = 0.4

VMEM = pl.BlockSpec(memory_space=pltpu.VMEM)
SMEM = pl.BlockSpec(memory_space=pltpu.SMEM)
F32 = jnp.float32
BF16 = jnp.bfloat16


def from_behind(value, axis, by):
    devices = lax.axis_size(axis)
    pairs = [(i, i + by) for i in range(devices) if 0 <= i + by < devices]
    return lax.ppermute(value, axis, pairs)


def sum_over_scen(value):
    devices = lax.axis_size("scen")
    total = value.astype(F32)
    for by in range(1, devices):
        pairs = [(i, (i + by) % devices) for i in range(devices)]
        total = total + lax.ppermute(value, "scen", pairs).astype(F32)
    return total


def per_step(shape):
    return pl.BlockSpec((shape[0] // STEPS,) + shape[1:], lambda i: (i, 0, 0))


def resident(shape):
    return pl.BlockSpec(shape, lambda i: (0, 0, 0))


def stepped_call(kernel, out_shape, in_specs, out_specs, flops, moved):
    return pl.pallas_call(
        kernel,
        grid=(STEPS,),
        out_shape=out_shape,
        in_specs=in_specs,
        out_specs=out_specs,
        compiler_params=pltpu.CompilerParams(vmem_limit_bytes=48 * 2**20),
        cost_estimate=pl.CostEstimate(flops=flops, bytes_accessed=moved, transcendentals=0),
    )


def rows_loop(count, step, unroll=UNROLL):
    unroll = max(u for u in range(1, unroll + 1) if count % u == 0)

    def chunk(c, carry):
        step([c * unroll + u for u in range(unroll)])
        return carry

    lax.fori_loop(0, count // unroll, chunk, 0)


def transposed_dot(a, b):
    return lax.dot_general(a, b, (((0,), (0,)), ((), ())), preferred_element_type=F32)


def zero_first(*refs):
    @pl.when(pl.program_id(0) == 0)
    def _():
        for ref in refs:
            ref[...] = jnp.zeros_like(ref)


def start_terms_kernel(live, right, tie, mu, terms, own):
    base = pl.program_id(0) * tie.shape[0]
    zero_first(own)

    def step(rows):
        parts = [transposed_dot(tie[j], (mu[j] * live[0]).astype(BF16)) for j in rows]
        for j, part in zip(rows, parts):
            terms[j] = part[BLK:].astype(BF16)
        for j, part in zip(rows, parts):
            own[right[base + j]] += part[:BLK]

    rows_loop(tie.shape[0], step)


def recourse_kernel(count, pattern, link, coupling, lam, grad, grad_first):
    base = pl.program_id(0) * coupling.shape[0]
    zero_first(grad, grad_first)

    def step(rows):
        halves = [jnp.where(base + r < count[0], lam[r], 0.0).astype(BF16) for r in rows]
        parts = [transposed_dot(coupling[r], h) for r, h in zip(rows, halves)]
        for r, part in zip(rows, parts):
            for k in range(KW):
                grad[pattern[(base + r) * KW + k]] += part[k * BLK : (k + 1) * BLK]
            grad_first[link[base + r]] += part[KW * BLK :]

    rows_loop(coupling.shape[0], step)


def primal_kernel(left, received, grad, own, cost, second, second_next, second_bar, sent, total):
    total[...] = grad[...] + own[...]

    def add_step(rows):
        for j in rows:
            total[left[j]] += received[j].astype(F32)

    rows_loop(received.shape[0], add_step, 8)

    def move_step(rows):
        news = []
        for b in rows:
            now = second[b]
            new = jnp.maximum(now - primal_step * (cost[b] - total[b]), 0.0)
            news.append((new, (2.0 * new - now).astype(BF16)))
        for b, (new, bar) in zip(rows, news):
            second_next[b] = new
            second_bar[b] = bar

    rows_loop(second.shape[0], move_step, 8)

    def gather_step(rows):
        picked = [second_bar[left[j]] for j in rows]
        for j, block in zip(rows, picked):
            sent[j] = block

    rows_loop(received.shape[0], gather_step, 16)


def dual_kernel(count, pattern, link, coupling, bar, first, target, lam, lam_next):
    base = pl.program_id(0) * coupling.shape[0]

    def step(rows):
        news = []
        for r in rows:
            at = base + r
            gathered = [bar[pattern[at * KW + k]] for k in range(KW)] + [first[link[at]]]
            coupled = jnp.dot(coupling[r], jnp.concatenate(gathered, axis=0), preferred_element_type=F32)
            new = lam[r] + dual_step * (target[r] - coupled)
            news.append(jnp.where(at < count[0], new, 0.0))
        for r, new in zip(rows, news):
            lam_next[r] = new

    rows_loop(coupling.shape[0], step)


def tie_kernel(live, right, tie, bar, arrived, mu, mu_next, *more):
    base = pl.program_id(0) * tie.shape[0]
    if more:
        zero_first(more[1])

    def step(rows):
        news = []
        for j in rows:
            stacked = jnp.concatenate([bar[right[base + j]], arrived[j]], axis=0)
            product = jnp.dot(tie[j], stacked, preferred_element_type=F32)
            news.append((mu[j] - dual_step * product) * live[0])
        parts = [transposed_dot(tie[j], new.astype(BF16)) for j, new in zip(rows, news)] if more else []
        for j, new in zip(rows, news):
            mu_next[j] = new
        for j, part in zip(rows, parts):
            more[0][j] = part[BLK:].astype(BF16)
            more[1][right[base + j]] += part[:BLK]

    rows_loop(tie.shape[0], step)


def primal_call(left, received, grad, own, cost, second):
    shape = second.shape
    return pl.pallas_call(
        primal_kernel,
        out_shape=(
            jax.ShapeDtypeStruct(shape, F32),
            jax.ShapeDtypeStruct(shape, BF16),
            jax.ShapeDtypeStruct(received.shape, BF16),
        ),
        in_specs=[SMEM] + [VMEM] * 5,
        out_specs=(VMEM,) * 3,
        scratch_shapes=[pltpu.VMEM(shape, F32)],
        compiler_params=pltpu.CompilerParams(vmem_limit_bytes=48 * 2**20),
        cost_estimate=pl.CostEstimate(flops=10**7, bytes_accessed=25 * 10**6, transcendentals=0),
    )(left, received, grad, own, cost, second)


def body(
    coupling,
    tie_blocks,
    w_pattern,
    link_pattern,
    left_bounds,
    right_bounds,
    block_counts,
    commit_cost,
    dispatch_cost,
    demand,
    wind_error,
    commit_start,
    dispatch_start,
    dual_start,
    tie_start,
):
    scen_dev = dispatch_start.shape[2]
    scen_total = scen_dev * lax.axis_size("scen")
    second_shape = dispatch_start.shape
    tie_shape = tie_start.shape
    wide_shape = commit_start.shape + (scen_dev,)
    live = (lax.axis_index("net") < lax.axis_size("net") - 1).astype(F32).reshape(1)
    pattern = w_pattern.reshape(-1)
    cost = jnp.broadcast_to(dispatch_cost[:, :, None], second_shape)
    target = demand[:, :, None] + wind_error.astype(F32)
    first_now = commit_start
    second_now = dispatch_start
    dual_now = dual_start
    tie_now = tie_start
    second_f32 = jax.ShapeDtypeStruct(second_shape, F32)
    tie_f32 = jax.ShapeDtypeStruct(tie_shape, F32)
    tie_bf16 = jax.ShapeDtypeStruct(tie_shape, BF16)
    dual_f32 = jax.ShapeDtypeStruct(dual_start.shape, F32)
    ties, rows = per_step(tie_shape), per_step(dual_start.shape)
    tie_mats, row_mats = per_step(tie_blocks.shape), per_step(coupling.shape)
    seconds, wides = resident(second_shape), resident(wide_shape)
    terms, own = stepped_call(
        start_terms_kernel,
        (tie_bf16, second_f32),
        [SMEM, SMEM, tie_mats, ties],
        (ties, seconds),
        3 * 10**8,
        13 * 10**6,
    )(live, right_bounds, tie_blocks, tie_start)
    for iteration in range(ITERS):
        received = from_behind(terms, "net", 1)
        grad, grad_wide = stepped_call(
            recourse_kernel,
            (second_f32, jax.ShapeDtypeStruct(wide_shape, F32)),
            [SMEM] * 3 + [row_mats, rows],
            (seconds, wides),
            5 * 10**8,
            16 * 10**6,
        )(block_counts, pattern, link_pattern, coupling, dual_now)
        grad_first = sum_over_scen((jnp.sum(grad_wide, axis=2) / scen_total).astype(BF16))
        second_next, second_bar, sent = primal_call(left_bounds, received, grad, own, cost, second_now)
        sent, grad_first = lax.optimization_barrier((sent, grad_first))
        arrived = from_behind(sent, "net", -1)
        first_next = jnp.clip(first_now - first_step * (commit_cost - grad_first), 0.0, 1.0)
        first_bar = (2.0 * first_next - first_now).astype(BF16)
        first_wide = jnp.broadcast_to(first_bar[:, :, None], wide_shape)
        dual_now = stepped_call(
            dual_kernel,
            dual_f32,
            [SMEM] * 3 + [row_mats, seconds, wides, rows, rows],
            rows,
            5 * 10**8,
            18 * 10**6,
        )(block_counts, pattern, link_pattern, coupling, second_bar, first_wide, target, dual_now)
        arrived, dual_now = lax.optimization_barrier((arrived, dual_now))
        more = iteration < ITERS - 1
        got = stepped_call(
            tie_kernel,
            (tie_f32, tie_bf16, second_f32) if more else (tie_f32,),
            [SMEM, SMEM, tie_mats, seconds, ties, ties],
            (ties, ties, seconds) if more else (ties,),
            6 * 10**8,
            18 * 10**6,
        )(live, right_bounds, tie_blocks, second_bar, arrived, tie_now)
        tie_now = got[0]
        if more:
            terms, own = got[1:]
        first_now = first_next
        second_now = second_next
    return (first_now, second_now, dual_now, tie_now)


def solution(mesh):
    return jax.shard_map(
        body,
        mesh=mesh,
        in_specs=(
            P("net", None, None),
            P("net", None, None),
            P("net", None),
            P("net"),
            P("net"),
            P("net"),
            P("net"),
            P("net", None),
            P("net", None),
            P("net", None),
            P("net", None, "scen"),
            P("net", None),
            P("net", None, "scen"),
            P("net", None, "scen"),
            P("net", None, "scen"),
        ),
        out_specs=(
            P("net", None),
            P("net", None, "scen"),
            P("net", None, "scen"),
            P("net", None, "scen"),
        ),
        check_vma=False,
    )
```

```python
import jax
import jax.numpy as jnp
from jax import lax
from jax.experimental import pallas as pl
from jax.experimental.pallas import tpu as pltpu
from jax.sharding import PartitionSpec as P

BLK = 64
KW = 4
ITERS = 2
UNROLL = 32
STEPS = 4

primal_step = 0.4
first_step = 1.0
dual_step = 0.4

VMEM = pl.BlockSpec(memory_space=pltpu.VMEM)
SMEM = pl.BlockSpec(memory_space=pltpu.SMEM)
F32 = jnp.float32
BF16 = jnp.bfloat16


def from_behind(value, axis, by):
    devices = lax.axis_size(axis)
    pairs = [(i, i + by) for i in range(devices) if 0 <= i + by < devices]
    return lax.ppermute(value, axis, pairs)


def sum_over_scen(value):
    devices = lax.axis_size("scen")
    total = value.astype(F32)
    for by in range(1, devices):
        pairs = [(i, (i + by) % devices) for i in range(devices)]
        total = total + lax.ppermute(value, "scen", pairs).astype(F32)
    return total


def per_step(shape):
    return pl.BlockSpec((shape[0] // STEPS,) + shape[1:], lambda i: (i, 0, 0))


def resident(shape):
    return pl.BlockSpec(shape, lambda i: (0, 0, 0))


def stepped_call(kernel, out_shape, in_specs, out_specs, flops, moved):
    return pl.pallas_call(
        kernel,
        grid=(STEPS,),
        out_shape=out_shape,
        in_specs=in_specs,
        out_specs=out_specs,
        compiler_params=pltpu.CompilerParams(vmem_limit_bytes=48 * 2**20),
        cost_estimate=pl.CostEstimate(flops=flops, bytes_accessed=moved, transcendentals=0),
    )


def rows_loop(count, step, unroll=UNROLL):
    unroll = max(u for u in range(1, unroll + 1) if count % u == 0)

    def chunk(c, carry):
        step([c * unroll + u for u in range(unroll)])
        return carry

    lax.fori_loop(0, count // unroll, chunk, 0)


def transposed_dot(a, b):
    return lax.dot_general(a, b, (((0,), (0,)), ((), ())), preferred_element_type=F32)


def zero_first(*refs):
    @pl.when(pl.program_id(0) == 0)
    def _():
        for ref in refs:
            ref[...] = jnp.zeros_like(ref)


def start_terms_kernel(live, right, tie, mu, terms, own):
    base = pl.program_id(0) * tie.shape[0]
    zero_first(own)

    def step(rows):
        parts = [transposed_dot(tie[j], (mu[j] * live[0]).astype(BF16)) for j in rows]
        for j, part in zip(rows, parts):
            terms[j] = part[BLK:].astype(BF16)
        for j, part in zip(rows, parts):
            own[right[base + j]] += part[:BLK]

    rows_loop(tie.shape[0], step)


def recourse_kernel(count, pattern, link, coupling, lam, grad, grad_first):
    base = pl.program_id(0) * coupling.shape[0]
    zero_first(grad, grad_first)

    def step(rows):
        halves = [jnp.where(base + r < count[0], lam[r], 0.0).astype(BF16) for r in rows]
        parts = [transposed_dot(coupling[r], h) for r, h in zip(rows, halves)]
        for r, part in zip(rows, parts):
            for k in range(KW):
                grad[pattern[(base + r) * KW + k]] += part[k * BLK : (k + 1) * BLK]
            grad_first[link[base + r]] += part[KW * BLK :]

    rows_loop(coupling.shape[0], step)


def primal_kernel(left, received, grad, own, cost, second, second_next, second_bar, sent, total):
    at = pl.program_id(0)
    zero_first(total)

    @pl.when(at < STEPS)
    def _():
        base = at * received.shape[0]

        def add_step(rows):
            for j in rows:
                total[left[base + j]] += received[j].astype(F32)

        rows_loop(received.shape[0], add_step, 8)

    @pl.when(at >= STEPS)
    def _():
        base = (at - STEPS) * second.shape[0]

        def move_step(rows):
            news = []
            for b in rows:
                now = second[b]
                slope = total[base + b] + grad[b] + own[b]
                new = jnp.maximum(now - primal_step * (cost[b] - slope), 0.0)
                news.append((new, (2.0 * new - now).astype(BF16)))
            for b, (new, bar) in zip(rows, news):
                second_next[b] = new
                second_bar[base + b] = bar

        rows_loop(second.shape[0], move_step, 8)

    @pl.when(at == 2 * STEPS - 1)
    def _():
        def gather_step(rows):
            picked = [second_bar[left[j]] for j in rows]
            for j, block in zip(rows, picked):
                sent[j] = block

        rows_loop(sent.shape[0], gather_step, 16)


def dual_kernel(count, pattern, link, coupling, bar, first, target, lam, lam_next):
    base = pl.program_id(0) * coupling.shape[0]

    def step(rows):
        news = []
        for r in rows:
            at = base + r
            gathered = [bar[pattern[at * KW + k]] for k in range(KW)] + [first[link[at]]]
            coupled = jnp.dot(coupling[r], jnp.concatenate(gathered, axis=0), preferred_element_type=F32)
            new = lam[r] + dual_step * (target[r] - coupled)
            news.append(jnp.where(at < count[0], new, 0.0))
        for r, new in zip(rows, news):
            lam_next[r] = new

    rows_loop(coupling.shape[0], step)


def tie_kernel(live, right, tie, bar, arrived, mu, mu_next, *more):
    base = pl.program_id(0) * tie.shape[0]
    if more:
        zero_first(more[1])

    def step(rows):
        news = []
        for j in rows:
            stacked = jnp.concatenate([bar[right[base + j]], arrived[j]], axis=0)
            product = jnp.dot(tie[j], stacked, preferred_element_type=F32)
            news.append((mu[j] - dual_step * product) * live[0])
        parts = [transposed_dot(tie[j], new.astype(BF16)) for j, new in zip(rows, news)] if more else []
        for j, new in zip(rows, news):
            mu_next[j] = new
        for j, part in zip(rows, parts):
            more[0][j] = part[BLK:].astype(BF16)
            more[1][right[base + j]] += part[:BLK]

    rows_loop(tie.shape[0], step)


def primal_call(left, received, grad, own, cost, second):
    shape = second.shape
    arriving = pl.BlockSpec(
        (received.shape[0] // STEPS,) + received.shape[1:], lambda i: (jnp.minimum(i, STEPS - 1), 0, 0)
    )
    moving = pl.BlockSpec((shape[0] // STEPS,) + shape[1:], lambda i: (jnp.maximum(i - STEPS, 0), 0, 0))
    return pl.pallas_call(
        primal_kernel,
        grid=(2 * STEPS,),
        out_shape=(
            jax.ShapeDtypeStruct(shape, F32),
            jax.ShapeDtypeStruct(shape, BF16),
            jax.ShapeDtypeStruct(received.shape, BF16),
        ),
        in_specs=[SMEM, arriving] + [moving] * 4,
        out_specs=(moving, resident(shape), resident(received.shape)),
        scratch_shapes=[pltpu.VMEM(shape, F32)],
        compiler_params=pltpu.CompilerParams(vmem_limit_bytes=48 * 2**20),
        cost_estimate=pl.CostEstimate(flops=10**7, bytes_accessed=25 * 10**6, transcendentals=0),
    )(left, received, grad, own, cost, second)


def body(
    coupling,
    tie_blocks,
    w_pattern,
    link_pattern,
    left_bounds,
    right_bounds,
    block_counts,
    commit_cost,
    dispatch_cost,
    demand,
    wind_error,
    commit_start,
    dispatch_start,
    dual_start,
    tie_start,
):
    scen_dev = dispatch_start.shape[2]
    scen_total = scen_dev * lax.axis_size("scen")
    second_shape = dispatch_start.shape
    tie_shape = tie_start.shape
    wide_shape = commit_start.shape + (scen_dev,)
    live = (lax.axis_index("net") < lax.axis_size("net") - 1).astype(F32).reshape(1)
    pattern = w_pattern.reshape(-1)
    target = demand[:, :, None] + wind_error.astype(F32)
    first_now = commit_start
    second_now = dispatch_start
    dual_now = dual_start
    tie_now = tie_start
    second_f32 = jax.ShapeDtypeStruct(second_shape, F32)
    tie_f32 = jax.ShapeDtypeStruct(tie_shape, F32)
    tie_bf16 = jax.ShapeDtypeStruct(tie_shape, BF16)
    dual_f32 = jax.ShapeDtypeStruct(dual_start.shape, F32)
    ties, rows = per_step(tie_shape), per_step(dual_start.shape)
    tie_mats, row_mats = per_step(tie_blocks.shape), per_step(coupling.shape)
    seconds, wides = resident(second_shape), resident(wide_shape)
    terms, own = stepped_call(
        start_terms_kernel,
        (tie_bf16, second_f32),
        [SMEM, SMEM, tie_mats, ties],
        (ties, seconds),
        3 * 10**8,
        13 * 10**6,
    )(live, right_bounds, tie_blocks, tie_start)
    terms, cost_rows = lax.optimization_barrier((terms, dispatch_cost))
    cost = jnp.broadcast_to(cost_rows[:, :, None], second_shape)
    cost, dual_now = lax.optimization_barrier((cost, dual_now))
    for iteration in range(ITERS):
        received = from_behind(terms, "net", 1)
        grad, grad_wide = stepped_call(
            recourse_kernel,
            (second_f32, jax.ShapeDtypeStruct(wide_shape, F32)),
            [SMEM] * 3 + [row_mats, rows],
            (seconds, wides),
            5 * 10**8,
            16 * 10**6,
        )(block_counts, pattern, link_pattern, coupling, dual_now)
        grad_first = sum_over_scen((jnp.sum(grad_wide, axis=2) / scen_total).astype(BF16))
        second_next, second_bar, sent = primal_call(left_bounds, received, grad, own, cost, second_now)
        sent, grad_first = lax.optimization_barrier((sent, grad_first))
        arrived = from_behind(sent, "net", -1)
        first_next = jnp.clip(first_now - first_step * (commit_cost - grad_first), 0.0, 1.0)
        first_bar = (2.0 * first_next - first_now).astype(BF16)
        first_wide = jnp.broadcast_to(first_bar[:, :, None], wide_shape)
        dual_now = stepped_call(
            dual_kernel,
            dual_f32,
            [SMEM] * 3 + [row_mats, seconds, wides, rows, rows],
            rows,
            5 * 10**8,
            18 * 10**6,
        )(block_counts, pattern, link_pattern, coupling, second_bar, first_wide, target, dual_now)
        arrived, dual_now = lax.optimization_barrier((arrived, dual_now))
        more = iteration < ITERS - 1
        got = stepped_call(
            tie_kernel,
            (tie_f32, tie_bf16, second_f32) if more else (tie_f32,),
            [SMEM, SMEM, tie_mats, seconds, ties, ties],
            (ties, ties, seconds) if more else (ties,),
            6 * 10**8,
            18 * 10**6,
        )(live, right_bounds, tie_blocks, second_bar, arrived, tie_now)
        tie_now = got[0]
        if more:
            terms, own = got[1:]
        first_now = first_next
        second_now = second_next
    return (first_now, second_now, dual_now, tie_now)


def solution(mesh):
    return jax.shard_map(
        body,
        mesh=mesh,
        in_specs=(
            P("net", None, None),
            P("net", None, None),
            P("net", None),
            P("net"),
            P("net"),
            P("net"),
            P("net"),
            P("net", None),
            P("net", None),
            P("net", None),
            P("net", None, "scen"),
            P("net", None),
            P("net", None, "scen"),
            P("net", None, "scen"),
            P("net", None, "scen"),
        ),
        out_specs=(
            P("net", None),
            P("net", None, "scen"),
            P("net", None, "scen"),
            P("net", None, "scen"),
        ),
        check_vma=False,
    )
```
